256 devices in a mesh: dp: 16 (over z, core), tensor: 16 (over y, x).
Axes of the slice: x: 4, y: 4, z: 8, core: 2. Of those that a mesh axis runs over, the one named last changes fastest.
Arguments:
- inputs: bfloat16 [2048, 6144], P('dp'), may hold values from -16 to 16
- preact: bfloat16 [2048, 24576], P('dp', 'tensor'), may hold values from -8 to 8
- grad_act: bfloat16 [2048, 24576], P('dp', 'tensor'), may hold values from -80 to 80
- weight: bfloat16 [6144, 24576], P('dp', 'tensor'), may hold values from -0.078125 to 0.078125
Outputs:
- grad_input: bfloat16 [2048, 6144], P('dp')
- weight_grad: float32 [6144, 24576], P('dp', 'tensor')
- grad_amax: float32 [], replicated
The draws below stay inside these ranges and needn't reach their ends.
All inputs are finite; a program needn't handle non-finite values.
Results may differ from the reference program's by a relative error of at most 0.02.
Values may be sent and summed in bfloat16 or wider, within the bound.
No kernel may reach another device: no remote copies, remote signals or barrier semaphores. Data moves between devices by JAX's collectives and lax.ppermute only.
A program may use at most 192 MiB of HBM per device.

```python
import math
import jax
import jax.numpy as jnp
from jax import lax

D = 6144
FF = 24576
TOK_DEV = 128
TOKENS = 2048
FF_DEV = 1536
REPLICAS = 16
BLOCKS = 16


def draw_inputs(key, part):
    key = jax.random.fold_in(key, 11)
    keys = jax.random.split(key, 2)
    base = jnp.clip(jax.random.normal(keys[0], (TOKENS, D), jnp.float32), -5.0, 5.0)
    col_scale = jnp.exp(jax.random.uniform(keys[1], (1, D), jnp.float32, math.log(0.4), math.log(2.5)))
    return (base * col_scale).astype(jnp.bfloat16)


def draw_grad_act(key, part):
    key = jax.random.fold_in(key, 7)
    keys = jax.random.split(key, 3)
    position = jnp.arange(TOKENS, dtype=jnp.float32) / max(TOKENS - 1, 1)
    row_jitter = jnp.exp(jax.random.uniform(keys[1], (TOKENS, 1), jnp.float32, 0.0, math.log(3.3)))
    col_scale = jnp.exp(jax.random.uniform(keys[2], (1, FF), jnp.float32, math.log(0.4), math.log(4.0)))
    base = jnp.clip(jax.random.normal(keys[0], (TOKENS, FF), jnp.float32), -5.0, 5.0)
    rising = jnp.exp(math.log(3.0) * position)
    return (0.15 * base * rising[:, None] * row_jitter * col_scale).astype(jnp.bfloat16)


def levels(own_key, dims, shards, smallest, high):
    loudness, own = 1.0, jax.random.fold_in(own_key, 6)
    for axis_at, parts in shards:
        heights = jnp.exp(jax.random.uniform(jax.random.fold_in(own, axis_at), (parts,), jnp.float32, smallest / len(shards), high / len(shards)))
        loudness = loudness * jnp.repeat(heights, dims[axis_at] // parts).reshape([-1 if axis == axis_at else 1 for axis in range(len(dims))])
    return loudness


def centred(rng, extent, width, most, cuts=(), kind=jnp.bfloat16):
    entries = jax.random.normal(rng, extent, jnp.float32) * width
    if len(cuts) > 0:
        entries = levels(rng, extent, cuts, -0.22, 0.18) * entries
    return jnp.clip(entries, min=-most, max=most).astype(kind)


def setup_inputs(seed: int = 0) -> dict:
    seeds = jax.random.split(jax.random.key(seed), 5)
    inputs = draw_inputs(jax.random.fold_in(seeds[4], 71), 0)
    preact = centred(seeds[1], (TOKENS, FF), 1.5, 8.0, ((0, 16), (1, 16)))
    grad_act = draw_grad_act(jax.random.fold_in(seeds[4], 71), 0)
    weight = centred(seeds[3], (D, FF), D ** -0.5, 0.078125, ((0, 16), (1, 16)))
    return {"inputs": inputs, "preact": preact, "grad_act": grad_act, "weight": weight}


gelu_coeff = math.sqrt(2.0 / math.pi)
epsilon = 1e-06

def slope_of(preact):
    values = preact.astype(jnp.float32)
    inner_arg = gelu_coeff * (values + 0.044715 * values * values * values)
    tanh_val = jnp.tanh(inner_arg)
    return 0.5 * (1.0 + tanh_val) + 0.5 * values * (1.0 - tanh_val * tanh_val) * gelu_coeff * (1.0 + 3.0 * 0.044715 * values * values)

def to_wire(values):
    return lax.optimization_barrier(values.astype(jnp.bfloat16)).astype(jnp.float32)

def reference(inputs, preact, grad_act, weight):
    grad_pre = (grad_act.astype(jnp.float32) * slope_of(preact)).astype(jnp.bfloat16)

    def block_step(running_sum, block_index):
        columns = lax.dynamic_slice_in_dim(grad_pre, block_index * FF_DEV, FF_DEV, 1)
        weight_cols = lax.dynamic_slice_in_dim(weight, block_index * FF_DEV, FF_DEV, 1)
        block_part = lax.dot_general(columns, weight_cols, (((1,), (1,)), ((), ())), preferred_element_type=jnp.float32)
        return (running_sum + to_wire(block_part), None)
    running_sum, _ = lax.scan(block_step, jnp.zeros((TOKENS, D), jnp.float32), jnp.arange(BLOCKS, dtype=jnp.int32))
    grad_input = running_sum.astype(jnp.bfloat16)

    def partial_of(replica):
        rows_in = lax.dynamic_slice_in_dim(inputs, replica * TOK_DEV, TOK_DEV, 0)
        rows_grad = lax.dynamic_slice_in_dim(grad_pre, replica * TOK_DEV, TOK_DEV, 0)
        return lax.dot_general(rows_in, rows_grad, (((0,), (0,)), ((), ())), preferred_element_type=jnp.float32)

    def max_step(largest, replica):
        return (jnp.maximum(largest, jnp.max(jnp.abs(partial_of(replica)))), None)
    replicas_idx = jnp.arange(REPLICAS, dtype=jnp.int32)
    grad_amax, _ = lax.scan(max_step, jnp.zeros((), jnp.float32), replicas_idx)
    grad_scale = 1.0 / (grad_amax + epsilon)

    def sum_step(accum, replica):
        return (accum + to_wire(partial_of(replica) * grad_scale), None)
    weight_grad, _ = lax.scan(sum_step, jnp.zeros((D, FF), jnp.float32), replicas_idx)
    return (grad_input, weight_grad, grad_amax)
```

```python
import functools
import math

import jax
import jax.numpy as jnp
from jax import lax
from jax.experimental import pallas as pl
from jax.experimental.pallas import tpu as pltpu
from jax.sharding import PartitionSpec as P

gelu_coeff = math.sqrt(2.0 / math.pi)
epsilon = 1e-06

D, FF_DEV, TOK_DEV = 6144, 1536, 128
NZ, NT = 8, 16
HALF = TOK_DEV // 2
OWN = D // 16
CHIP = 2 * OWN
WIDE = CHIP + 128

VMEM = pl.BlockSpec(memory_space=pltpu.VMEM)
SMEM = pl.BlockSpec(memory_space=pltpu.SMEM)


def params(mib=48):
    return pltpu.CompilerParams(vmem_limit_bytes=mib << 20)


def dot(left, right, left_dim, right_dim):
    return lax.dot_general(
        left, right, (((left_dim,), (right_dim,)), ((), ())), preferred_element_type=jnp.float32
    )


def dev(z, c, t):
    return ((z % NZ) * 2 + c) * NT + t


def ring_perm(step):
    return [(z * 2 + c, ((z + step * (1 - 2 * c)) % NZ) * 2 + c) for z in range(NZ) for c in range(2)]


CORE_SWAP = [(d, d ^ 1) for d in range(2 * NZ)]


def spread_perm(sign):
    return [
        (dev(z, c, t), dev(z + sign * (1 - 2 * c) * (t >> 1), c, t))
        for z in range(NZ)
        for c in range(2)
        for t in range(NT)
    ]


def slope_kernel(pre_ref, act_ref, first_ref, second_ref):
    values = pre_ref[...].astype(jnp.float32)
    inner_arg = gelu_coeff * (values + 0.044715 * values * values * values)
    tanh_val = jnp.tanh(inner_arg)
    slope = 0.5 * (1.0 + tanh_val) + 0.5 * values * (1.0 - tanh_val * tanh_val) * gelu_coeff * (
        1.0 + 3.0 * 0.044715 * values * values
    )
    grad = (act_ref[...].astype(jnp.float32) * slope).astype(jnp.bfloat16)
    first_ref[...] = grad[:HALF]
    second_ref[...] = grad[HALF:]


def amax_kernel(in_ref, first_ref, second_ref, out_ref, grad, best):
    step = pl.program_id(0)

    @pl.when(step == 0)
    def _():
        grad[:HALF] = first_ref[...]
        grad[HALF:] = second_ref[...]
        best[...] = jnp.zeros_like(best)

    product = jnp.abs(dot(grad[...], in_ref[...], 0, 0))
    rows, cols = product.shape
    best[...] = jnp.maximum(best[...], jnp.max(product.reshape(rows // 8, 8, cols), axis=0))

    @pl.when(step == pl.num_programs(0) - 1)
    def _():
        out_ref[...] = jnp.full(out_ref.shape, jnp.max(best[...]), jnp.float32)


def block_kernel(*refs):
    chunks, (own_w, other_w, amax_ref, amax_other, out_ref, rows) = refs[:NT], refs[NT:]
    for n in range(NT):
        rows[n * HALF : (n + 1) * HALF] = chunks[n][...]
    for j, w in enumerate((own_w, other_w)):
        for part in range(2):
            span = pl.ds(part * 512, 512)
            product = dot(rows[span, :], w[...], 1, 1).astype(jnp.bfloat16)
            out_ref[part * 8 : part * 8 + 8, :, j * OWN : (j + 1) * OWN] = product.reshape(8, HALF, OWN)
    most = jnp.maximum(amax_ref[...], amax_other[...])[:1]
    high = most.astype(jnp.bfloat16)
    rest = most - high.astype(jnp.float32)
    mid = rest.astype(jnp.bfloat16)
    low = (rest - mid.astype(jnp.float32)).astype(jnp.bfloat16)
    for n in range(NT):
        for at, piece in enumerate((high, mid, low, low)):
            out_ref[n, at * 16 : at * 16 + 16, CHIP:] = jnp.broadcast_to(piece, (16, 128))


def joined(pieces):
    parts = [pieces[..., at * 16 : at * 16 + 1, :].astype(jnp.float32) for at in range(3)]
    return (parts[0] + parts[1]) + parts[2]


def sum_kernel(in_ref, out_ref):
    total = in_ref[0, :, :CHIP].astype(jnp.float32)
    for n in range(1, NT):
        total = total + in_ref[n, :, :CHIP].astype(jnp.float32)
    out_ref[:, :CHIP] = total.astype(jnp.bfloat16)
    most = joined(in_ref[0, :, CHIP:])
    for n in range(1, NT):
        most = jnp.maximum(most, joined(in_ref[n, :, CHIP:]))
    high = most.astype(jnp.bfloat16)
    rest = most - high.astype(jnp.float32)
    mid = rest.astype(jnp.bfloat16)
    low = (rest - mid.astype(jnp.float32)).astype(jnp.bfloat16)
    for at, piece in enumerate((high, mid, low, low)):
        out_ref[at * 16 : at * 16 + 16, CHIP:] = jnp.broadcast_to(piece, (16, 128))


def outer_kernel(*refs):
    chunks, (in_ref, own_ref, other_ref, rows) = refs[:NT], refs[NT:]
    for n in range(NT):
        rows[n * HALF : (n + 1) * HALF] = chunks[n][...]
    left = in_ref[...].reshape(NT * HALF, CHIP)
    own_ref[...] = dot(left[:, :OWN], rows[...], 0, 0)
    other_ref[...] = dot(left[:, OWN:], rows[...], 0, 0).astype(jnp.bfloat16)


def place_kernel(at_ref, in_ref, out_ref, amax_ref):
    z, c = at_ref[0], at_ref[1]
    for k in range(NZ):
        chip = lax.rem(z + (1 - 2 * c) * k + NZ, NZ)
        for j in range(2):
            side = c if j == 0 else 1 - c
            start = pl.multiple_of((chip * 2 + side) * OWN, 128)
            for h in range(2):
                out_ref[h * HALF : (h + 1) * HALF, pl.ds(start, OWN)] = in_ref[2 * k + h, :, j * OWN : (j + 1) * OWN]
    most = joined(in_ref[0, :, CHIP:])
    for n in range(1, NT):
        most = jnp.maximum(most, joined(in_ref[n, :, CHIP:]))
    amax_ref[...] = jnp.broadcast_to(most, amax_ref.shape)


def scale_kernel(own_ref, come_ref, amax_ref, out_ref):
    scale = 1.0 / (amax_ref[:1, :1] + epsilon)
    out_ref[...] = (own_ref[...] + come_ref[...].astype(jnp.float32)) * scale


def shape(dims, kind=jnp.bfloat16):
    return jax.ShapeDtypeStruct(dims, kind)


def on_device(inputs, preact, grad_act, weight):
    d, t = lax.axis_index("dp"), lax.axis_index("tensor")
    z, c = d // 2, d % 2
    k, half = t // 2, t % 2
    chip = (z + (1 - 2 * c) * k) % NZ
    pieces = [
        lax.dynamic_slice(inputs, (half * HALF, (chip * 2 + side) * OWN), (HALF, OWN)) for side in (c, 1 - c)
    ]
    sent = lax.ppermute(jnp.concatenate(pieces, axis=1), ("dp", "tensor"), spread_perm(1))
    in_all = lax.all_gather(sent, "tensor", axis=0)

    first, second = pl.pallas_call(
        slope_kernel,
        in_specs=[VMEM] * 2,
        out_specs=[VMEM] * 2,
        out_shape=[shape((HALF, FF_DEV))] * 2,
        compiler_params=params(),
        name="slope",
    )(preact, grad_act)
    other_w = lax.ppermute(weight, "dp", CORE_SWAP)

    chunks = {(0, 0): first, (0, 1): second}
    for step in range(1, 5):
        for sign, h in ((1, 0), (-1, 0), (1, 1), (-1, 1)):
            if step == 4 and (sign, h) in ((-1, 0), (1, 1)):
                continue
            before = chunks[((sign * (step - 1)) % NZ, h)]
            chunks[((sign * step) % NZ, h)] = lax.ppermute(before, "dp", ring_perm(sign))
    rows = [chunks[(n // 2, n % 2)] for n in range(NT)]

    amax = pl.pallas_call(
        amax_kernel,
        grid=(12,),
        in_specs=[
            pl.BlockSpec((TOK_DEV, 512), lambda n: (0, n)),
            pl.BlockSpec((HALF, FF_DEV), lambda n: (0, 0)),
            pl.BlockSpec((HALF, FF_DEV), lambda n: (0, 0)),
        ],
        out_specs=pl.BlockSpec((8, 128), lambda n: (0, 0)),
        out_shape=shape((8, 128), jnp.float32),
        scratch_shapes=[pltpu.VMEM((TOK_DEV, FF_DEV), jnp.bfloat16), pltpu.VMEM((8, 512), jnp.float32)],
        compiler_params=params(),
        cost_estimate=pl.CostEstimate(flops=2 * TOK_DEV * FF_DEV * D, bytes_accessed=2 << 20, transcendentals=0),
        name="amax",
    )(inputs, first, second)
    amax_other = lax.ppermute(amax, "dp", CORE_SWAP)

    block = pl.pallas_call(
        block_kernel,
        in_specs=[VMEM] * (NT + 4),
        out_specs=VMEM,
        out_shape=shape((NT, HALF, WIDE)),
        scratch_shapes=[pltpu.VMEM((NT * HALF, FF_DEV), jnp.bfloat16)],
        compiler_params=params(),
        cost_estimate=pl.CostEstimate(flops=2 * 1024 * FF_DEV * CHIP, bytes_accessed=7 << 20, transcendentals=0),
        name="block",
    )(*rows, weight, other_w, amax, amax_other)
    swapped = lax.all_to_all(block, "tensor", 0, 0)
    summed = pl.pallas_call(
        sum_kernel,
        in_specs=[VMEM],
        out_specs=VMEM,
        out_shape=shape((HALF, WIDE)),
        compiler_params=params(),
        name="sum",
    )(swapped)
    back = lax.ppermute(summed, ("dp", "tensor"), spread_perm(-1))

    own, other = pl.pallas_call(
        outer_kernel,
        in_specs=[VMEM] * (NT + 1),
        out_specs=[VMEM] * 2,
        out_shape=[shape((OWN, FF_DEV), jnp.float32), shape((OWN, FF_DEV))],
        scratch_shapes=[pltpu.VMEM((NT * HALF, FF_DEV), jnp.bfloat16)],
        compiler_params=params(),
        cost_estimate=pl.CostEstimate(flops=2 * 1024 * FF_DEV * CHIP, bytes_accessed=9 << 20, transcendentals=0),
        name="outer",
    )(*rows, in_all)
    come = lax.ppermute(other, "dp", CORE_SWAP)

    whole = lax.all_to_all(jnp.broadcast_to(back[None], (NT, HALF, WIDE)), "tensor", 0, 0)
    grad_input, grad_amax = pl.pallas_call(
        place_kernel,
        in_specs=[SMEM, VMEM],
        out_specs=[VMEM] * 2,
        out_shape=[shape((TOK_DEV, D)), shape((8, 128), jnp.float32)],
        compiler_params=params(),
        name="place",
    )(jnp.stack([z, c]).astype(jnp.int32), whole)
    weight_grad = pl.pallas_call(
        scale_kernel,
        in_specs=[VMEM] * 3,
        out_specs=VMEM,
        out_shape=shape((OWN, FF_DEV), jnp.float32),
        compiler_params=params(),
        name="scale",
    )(own, come, grad_amax)
    return (grad_input, weight_grad, grad_amax[0, 0])


def solution(mesh):
    placed = (P("dp", None), P("dp", "tensor"), P("dp", "tensor"), P("dp", "tensor"))
    return jax.shard_map(
        on_device,
        mesh=mesh,
        in_specs=placed,
        out_specs=(P("dp", None), P("dp", "tensor"), P()),
        check_vma=False,
    )
```

```python
import functools
import math

import jax
import jax.numpy as jnp
from jax import lax
from jax.experimental import pallas as pl
from jax.experimental.pallas import tpu as pltpu
from jax.sharding import PartitionSpec as P

gelu_coeff = math.sqrt(2.0 / math.pi)
epsilon = 1e-06

D, FF_DEV, TOK_DEV = 6144, 1536, 128
NZ, NT = 8, 16
HALF = TOK_DEV // 2
OWN = D // 16
CHIP = 2 * OWN
LANES = 128
WIDE = CHIP + LANES

VMEM = pl.BlockSpec(memory_space=pltpu.VMEM)
HBM = pl.BlockSpec(memory_space=pltpu.HBM)
SMEM = pl.BlockSpec(memory_space=pltpu.SMEM)


def params(mib):
    return pltpu.CompilerParams(vmem_limit_bytes=mib << 20)


def dot(left, right, left_dim, right_dim):
    return lax.dot_general(
        left, right, (((left_dim,), (right_dim,)), ((), ())), preferred_element_type=jnp.float32
    )


def dev(z, c, t):
    return ((z % NZ) * 2 + c) * NT + t


def ring_perm(step):
    return [(z * 2 + c, ((z + step * (1 - 2 * c)) % NZ) * 2 + c) for z in range(NZ) for c in range(2)]


CORE_SWAP = [(d, d ^ 1) for d in range(2 * NZ)]


def shift_of(c, k):
    return k - 4 * c


def block_of(c, k):
    return lax.rem((1 - 2 * c) * k + 4 * c + NZ, NZ)


def spread_perm(sign):
    return [
        (dev(z, c, t), dev(z + sign * shift_of(c, t >> 1), c, t))
        for z in range(NZ)
        for c in range(2)
        for t in range(NT)
    ]


def fetch(pairs, sems):
    copies = [pltpu.make_async_copy(src, dst, sems.at[n]) for n, (src, dst) in enumerate(pairs)]
    for copy in copies:
        copy.start()
    return copies


def slope_kernel(pre_hbm, act_hbm, first_ref, second_ref, pre, act, sems):
    for copy in fetch([(pre_hbm, pre), (act_hbm, act)], sems):
        copy.wait()
    values = pre[...].astype(jnp.float32)
    inner_arg = gelu_coeff * (values + 0.044715 * values * values * values)
    tanh_val = jnp.tanh(inner_arg)
    slope = 0.5 * (1.0 + tanh_val) + 0.5 * values * (1.0 - tanh_val * tanh_val) * gelu_coeff * (
        1.0 + 3.0 * 0.044715 * values * values
    )
    grad = (act[...].astype(jnp.float32) * slope).astype(jnp.bfloat16)
    first_ref[...] = grad[:HALF]
    second_ref[...] = grad[HALF:]


def pieces_of(most):
    high = most.astype(jnp.bfloat16).astype(jnp.float32)
    mid = (most - high).astype(jnp.bfloat16).astype(jnp.float32)
    low = (most - high) - mid
    row = lax.broadcasted_iota(jnp.int32, (16, LANES), 0)
    return jnp.where(row == 0, high, jnp.where(row == 1, mid, low)).astype(jnp.bfloat16)


def joined(pieces):
    wide = pieces.astype(jnp.float32)
    return (wide[..., 0:1, :] + wide[..., 1:2, :]) + wide[..., 2:3, :]


def amax_kernel(part, before_ref, in_ref, first_ref, second_ref, out_ref):
    width = D // AMAX_PARTS
    best = jnp.zeros((8, 256), jnp.float32)
    for i in range(FF_DEV // 256):
        span = slice(i * 256, (i + 1) * 256)
        left = jnp.concatenate([first_ref[:, span], second_ref[:, span]], axis=0).T
        for j in range(width // 256):
            features = in_ref[:, part * width + j * 256 : part * width + (j + 1) * 256]
            product = jnp.abs(dot(left, features, 1, 0))
            best = jnp.maximum(best, jnp.max(product.reshape(32, 8, 256), axis=0))
    out_ref[...] = jnp.maximum(before_ref[...], jnp.max(best))


def pick_kernel(at_ref, in_hbm, *refs):
    outs, (tokens, made, sems) = refs[:NZ], refs[NZ:]
    z, c, h = at_ref[0], at_ref[1], at_ref[2]
    load = pltpu.make_async_copy(in_hbm.at[pl.ds(pl.multiple_of(h * HALF, HALF), HALF)], tokens, sems.at[NZ])
    load.start()
    load.wait()
    sent = []
    for k in range(NZ):
        chip = lax.rem(z + (1 - 2 * c) * k + NZ, NZ)
        for j in range(2):
            side = c if j == 0 else 1 - c
            start = pl.multiple_of((chip * 2 + side) * OWN, LANES)
            made[k, :, j * OWN : (j + 1) * OWN] = tokens[:, pl.ds(start, OWN)]
        sent.append(pltpu.make_async_copy(made.at[k], outs[k], sems.at[k]))
        sent[-1].start()
    for copy in sent:
        copy.wait()


def stack_kernel(*refs):
    pieces, (out_ref, token_ref, sems) = refs[:NZ], refs[NZ:]
    copies = fetch([(piece, out_ref.at[k]) for k, piece in enumerate(pieces)], sems)
    token_ref[...] = jnp.zeros_like(token_ref)
    for copy in copies:
        copy.wait()


def tie_kernel(*refs):
    pass


def gate_kernel(*refs):
    refs[-1][...] = jnp.zeros_like(refs[-1])


def block_kernel(*refs):
    at_ref, chunks = refs[0], refs[1 : NT + 1]
    own_w, other_w, amax_ref, amax_other, out_hbm, rows, weights, made, sems, out_sems = refs[NT + 1 :]
    c = at_ref[1]
    copies = fetch(
        [(own_w, weights.at[0])]
        + [(chunk, rows.at[pl.ds(n * HALF, HALF)]) for n, chunk in enumerate(chunks)]
        + [(other_w, weights.at[1])],
        sems,
    )
    lanes = pieces_of(jnp.maximum(amax_ref[...], amax_other[...])[:1])
    for n in range(NT):
        for q in range(HALF // 16):
            made[n, q * 16 : q * 16 + 16, CHIP:] = lanes
    outs = []
    for j in range(2):
        copies[j * (NT + 1)].wait()
        for group in range(4):
            if j == 0:
                for n in range(4 * group, 4 * group + 4):
                    copies[1 + n].wait()
            left = rows[4 * group * HALF : 4 * (group + 1) * HALF]
            product = dot(left, weights[j], 1, 1).astype(jnp.bfloat16).reshape(4, HALF, OWN)
            made[4 * group : 4 * group + 4, :, j * OWN : (j + 1) * OWN] = product
            if j == 0:
                continue
            for k in (2 * group, 2 * group + 1):
                there = out_hbm.at[pl.ds(2 * block_of(c, k), 2)]
                outs.append(pltpu.make_async_copy(made.at[pl.ds(2 * k, 2)], there, out_sems.at[k]))
                outs[-1].start()
    for copy in outs:
        copy.wait()


def sum_kernel(in_ref, _, out_ref):
    total = in_ref[0, :, :CHIP].astype(jnp.float32)
    for n in range(1, NT):
        total = total + in_ref[n, :, :CHIP].astype(jnp.float32)
    out_ref[:, :CHIP] = total.astype(jnp.bfloat16)
    most = joined(in_ref[0, :16, CHIP:])
    for n in range(1, NT):
        most = jnp.maximum(most, joined(in_ref[n, :16, CHIP:]))
    for q in range(HALF // 16):
        out_ref[q * 16 : q * 16 + 16, CHIP:] = pieces_of(most)


def spread_kernel(in_ref, _, out_ref, token_ref):
    for n in range(NT):
        out_ref[n] = in_ref[...]
    token_ref[...] = jnp.zeros_like(token_ref)


def outer_kernel(at_ref, _, *refs):
    chunks = refs[:NT]
    mine_ref, theirs_ref, own_ref, other_ref, rows, left = refs[NT:]
    for n in range(NT):
        rows[n * HALF : (n + 1) * HALF] = chunks[n][...]
    for h, (one, two) in enumerate(((mine_ref, theirs_ref), (theirs_ref, mine_ref))):

        @pl.when(at_ref[2] == h)
        def _(one=one, two=two):
            for k in range(NZ):
                left[k * TOK_DEV : k * TOK_DEV + HALF] = one[k]
                left[k * TOK_DEV + HALF : (k + 1) * TOK_DEV] = two[k]

    other_ref[...] = dot(left[:, OWN:], rows[...], 0, 0).astype(jnp.bfloat16)
    own_ref[...] = dot(left[:, :OWN], rows[...], 0, 0).astype(jnp.bfloat16)


def final_kernel(
    at_ref, whole_hbm, own_hbm, come_hbm, gi_hbm, wg_hbm, amax_ref, whole, gi, own, come, made, sems
):
    whole_in, own_in, come_in = fetch([(whole_hbm, whole), (own_hbm, own), (come_hbm, come)], sems)
    z, c = at_ref[0], at_ref[1]
    whole_in.wait()
    most = joined(whole[0, :16, CHIP:])
    for n in range(1, NT):
        most = jnp.maximum(most, joined(whole[n, :16, CHIP:]))
    amax_ref[0, 0] = jnp.max(most)
    for k in range(NZ):
        chip = lax.rem(z + shift_of(c, k) + NZ, NZ)
        for j in range(2):
            side = c if j == 0 else 1 - c
            start = pl.multiple_of((chip * 2 + side) * OWN, LANES)
            for h in range(2):
                gi[h * HALF : (h + 1) * HALF, pl.ds(start, OWN)] = whole[2 * k + h, :, j * OWN : (j + 1) * OWN]
    outs = [pltpu.make_async_copy(gi, gi_hbm, sems.at[6])]
    outs[0].start()
    scale = 1.0 / (most[:, :1] + epsilon)
    own_in.wait()
    come_in.wait()
    for n in range(4):
        span = pl.ds(n * (OWN // 4), OWN // 4)
        made[span, :] = (own[span, :].astype(jnp.float32) + come[span, :].astype(jnp.float32)) * scale
        outs.append(pltpu.make_async_copy(made.at[span], wg_hbm.at[span], sems.at[2 + n]))
        outs[-1].start()
    for copy in outs:
        copy.wait()


def shape(dims, kind=jnp.bfloat16):
    return jax.ShapeDtypeStruct(dims, kind)


def cost(flops, moved):
    return pl.CostEstimate(flops=flops, bytes_accessed=moved, transcendentals=0)


def dma(count):
    return pltpu.SemaphoreType.DMA((count,))


AMAX_PARTS = 4


def call(kernel, in_specs, out_specs, out_shape, name, scratch=(), flops=0, moved=1 << 20, mib=56, **more):
    return pl.pallas_call(
        kernel,
        in_specs=in_specs,
        out_specs=out_specs,
        out_shape=out_shape,
        scratch_shapes=list(scratch),
        compiler_params=params(mib),
        cost_estimate=cost(flops, moved),
        name=name,
        **more,
    )


def tie(arrays, mib=4):
    count = len(arrays)
    return call(
        tie_kernel,
        [HBM] * count,
        [HBM] * count,
        [shape(array.shape, array.dtype) for array in arrays],
        "tie",
        mib=mib,
        input_output_aliases={n: n for n in range(count)},
    )(*arrays)


def gate(arrays):
    return call(gate_kernel, [HBM] * len(arrays), VMEM, shape((8, 128), jnp.float32), "gate")(*arrays)


def on_device(inputs, preact, grad_act, weight):
    d, t = lax.axis_index("dp"), lax.axis_index("tensor")
    place = jnp.stack([d // 2, d % 2, t % 2]).astype(jnp.int32)
    tile = shape((8, 128), jnp.float32)

    first, second = call(
        slope_kernel,
        [HBM] * 2,
        [VMEM] * 2,
        [shape((HALF, FF_DEV))] * 2,
        "slope",
        [pltpu.VMEM((TOK_DEV, FF_DEV), jnp.bfloat16)] * 2 + [dma(2)],
    )(preact, grad_act)
    other_w = lax.ppermute(weight, "dp", CORE_SWAP)

    chunks = {0: first, 1: second}

    def step(steps, h, *after):
        at = [((sign * (steps - 1)) % NZ) * 2 + h for sign in (1, -1)]
        if after:
            held = tie([chunks[n] for n in at] + list(after))
            chunks.update(zip(at, held))
            after = held[2:]
        for sign, n in zip((1, -1), at):
            if steps == 4 and (sign, h) in ((-1, 0), (1, 1)):
                continue
            chunks[((sign * steps) % NZ) * 2 + h] = lax.ppermute(chunks[n], "dp", ring_perm(sign))
        return after

    def amax_part(part, before):
        return call(
            functools.partial(amax_kernel, part),
            [VMEM] * 4,
            VMEM,
            tile,
            "amax",
            flops=2 * TOK_DEV * FF_DEV * D // AMAX_PARTS,
            mib=8,
        )(before, inputs, first, second)

    step(1, 0)
    step(1, 1)
    amax = amax_part(0, jnp.zeros((8, 128), jnp.float32))
    (amax,) = step(2, 0, amax)
    amax = amax_part(1, amax)
    (amax,) = step(2, 1, amax)
    amax = amax_part(2, amax)
    (amax,) = step(3, 0, amax)
    amax = amax_part(3, amax)
    (amax,) = step(3, 1, amax)
    amax_other = lax.ppermute(amax, "dp", CORE_SWAP)
    step(4, 0)
    step(4, 1)

    block = call(
        block_kernel,
        [SMEM] + [HBM] * (NT + 2) + [VMEM] * 2,
        HBM,
        shape((NT, HALF, WIDE)),
        "block",
        [
            pltpu.VMEM((NT * HALF, FF_DEV), jnp.bfloat16),
            pltpu.VMEM((2, OWN, FF_DEV), jnp.bfloat16),
            pltpu.VMEM((NT, HALF, WIDE), jnp.bfloat16),
            dma(NT + 2),
            dma(2 * NZ),
        ],
        2 * 1024 * FF_DEV * CHIP,
        7 << 20,
    )(place, *[chunks[n] for n in range(NT)], weight, other_w, amax, amax_other)
    swapped = lax.all_to_all(block, "tensor", 0, 0)

    pieces = call(
        pick_kernel,
        [SMEM, HBM],
        [HBM] * NZ,
        [shape((HALF, CHIP))] * NZ,
        "pick",
        [pltpu.VMEM((HALF, D), jnp.bfloat16), pltpu.VMEM((NZ, HALF, CHIP), jnp.bfloat16), dma(NZ + 1)],
    )(place, inputs)
    come_in = {0: pieces[0]}
    for k in (1, 7, 2, 6, 3, 5, 4):
        come_in[k] = lax.ppermute(pieces[k], "dp", ring_perm(k))
    mine, here = call(
        stack_kernel,
        [HBM] * NZ,
        [VMEM] * 2,
        [shape((NZ, HALF, CHIP)), tile],
        "stack",
        [dma(NZ)],
    )(*[come_in[k] for k in range(NZ)])
    theirs = lax.ppermute(mine, "tensor", [(n, n ^ 1) for n in range(NT)])
    summed = call(sum_kernel, [VMEM] * 2, VMEM, shape((HALF, WIDE)), "sum", mib=16)(swapped, here)
    back = lax.ppermute(summed, ("dp", "tensor"), spread_perm(-1))

    copies, token = call(
        spread_kernel, [VMEM] * 2, [VMEM] * 2, [shape((NT, HALF, WIDE)), tile], "spread", mib=16
    )(back, here)
    whole = lax.all_to_all(copies, "tensor", 0, 0)
    own, other = call(
        outer_kernel,
        [SMEM, VMEM] + [VMEM] * (NT + 2),
        [VMEM] * 2,
        [shape((OWN, FF_DEV))] * 2,
        "outer",
        [pltpu.VMEM((NT * HALF, FF_DEV), jnp.bfloat16), pltpu.VMEM((NT * HALF, CHIP), jnp.bfloat16)],
        2 * 1024 * FF_DEV * CHIP,
        9 << 20,
        mib=48,
    )(place, token, *[chunks[n] for n in range(NT)], mine, theirs)
    come = lax.ppermute(other, "dp", CORE_SWAP)
    grad_input, weight_grad, grad_amax = call(
        final_kernel,
        [SMEM, HBM, HBM, HBM],
        [HBM, HBM, SMEM],
        [shape((TOK_DEV, D)), shape((OWN, FF_DEV), jnp.float32), shape((1, 1), jnp.float32)],
        "final",
        [
            pltpu.VMEM((NT, HALF, WIDE), jnp.bfloat16),
            pltpu.VMEM((TOK_DEV, D), jnp.bfloat16),
            pltpu.VMEM((OWN, FF_DEV), jnp.bfloat16),
            pltpu.VMEM((OWN, FF_DEV), jnp.bfloat16),
            pltpu.VMEM((OWN, FF_DEV), jnp.float32),
            dma(7),
        ],
    )(place, whole, own, come)
    return (grad_input, weight_grad, grad_amax.reshape(()))


def solution(mesh):
    placed = (P("dp", None), P("dp", "tensor"), P("dp", "tensor"), P("dp", "tensor"))
    return jax.shard_map(
        on_device,
        mesh=mesh,
        in_specs=placed,
        out_specs=(P("dp", None), P("dp", "tensor"), P()),
        check_vma=False,
    )
```

```python
import functools
import math

import jax
import jax.numpy as jnp
from jax import lax
from jax.experimental import pallas as pl
from jax.experimental.pallas import tpu as pltpu
from jax.sharding import PartitionSpec as P

gelu_coeff = math.sqrt(2.0 / math.pi)
epsilon = 1e-06

D, FF_DEV, TOK_DEV = 6144, 1536, 128
NZ, NT = 8, 16
HALF = TOK_DEV // 2
OWN = D // 16
CHIP = 2 * OWN
LANES = 128
WIDE = CHIP + LANES

VMEM = pl.BlockSpec(memory_space=pltpu.VMEM)
HBM = pl.BlockSpec(memory_space=pltpu.HBM)
SMEM = pl.BlockSpec(memory_space=pltpu.SMEM)


def params(mib):
    return pltpu.CompilerParams(vmem_limit_bytes=mib << 20)


def dot(left, right, left_dim, right_dim):
    return lax.dot_general(
        left, right, (((left_dim,), (right_dim,)), ((), ())), preferred_element_type=jnp.float32
    )


def dev(z, c, t):
    return ((z % NZ) * 2 + c) * NT + t


def ring_perm(step):
    return [(z * 2 + c, ((z + step * (1 - 2 * c)) % NZ) * 2 + c) for z in range(NZ) for c in range(2)]


CORE_SWAP = [(d, d ^ 1) for d in range(2 * NZ)]


def shift_of(c, k):
    return k - 4 * c


def block_of(c, k):
    return lax.rem((1 - 2 * c) * k + 4 * c + NZ, NZ)


def spread_perm(sign):
    return [
        (dev(z, c, t), dev(z + sign * shift_of(c, t >> 1), c, t))
        for z in range(NZ)
        for c in range(2)
        for t in range(NT)
    ]


def fetch(pairs, sems):
    copies = [pltpu.make_async_copy(src, dst, sems.at[n]) for n, (src, dst) in enumerate(pairs)]
    for copy in copies:
        copy.start()
    return copies


def slope_kernel(pre_hbm, act_hbm, first_ref, second_ref, pre, act, sems):
    for copy in fetch([(pre_hbm, pre), (act_hbm, act)], sems):
        copy.wait()
    values = pre[...].astype(jnp.float32)
    inner_arg = gelu_coeff * (values + 0.044715 * values * values * values)
    tanh_val = jnp.tanh(inner_arg)
    slope = 0.5 * (1.0 + tanh_val) + 0.5 * values * (1.0 - tanh_val * tanh_val) * gelu_coeff * (
        1.0 + 3.0 * 0.044715 * values * values
    )
    grad = (act[...].astype(jnp.float32) * slope).astype(jnp.bfloat16)
    first_ref[...] = grad[:HALF]
    second_ref[...] = grad[HALF:]


def pieces_of(most):
    high = most.astype(jnp.bfloat16).astype(jnp.float32)
    mid = (most - high).astype(jnp.bfloat16).astype(jnp.float32)
    low = (most - high) - mid
    row = lax.broadcasted_iota(jnp.int32, (16, LANES), 0)
    return jnp.where(row == 0, high, jnp.where(row == 1, mid, low)).astype(jnp.bfloat16)


def joined(pieces):
    wide = pieces.astype(jnp.float32)
    return (wide[..., 0:1, :] + wide[..., 1:2, :]) + wide[..., 2:3, :]


def amax_kernel(part, before_ref, in_ref, first_ref, second_ref, out_ref):
    width = D // AMAX_PARTS
    best = jnp.zeros((8, 256), jnp.float32)
    for i in range(FF_DEV // 256):
        span = slice(i * 256, (i + 1) * 256)
        left = jnp.concatenate([first_ref[:, span], second_ref[:, span]], axis=0).T
        for j in range(width // 256):
            features = in_ref[:, part * width + j * 256 : part * width + (j + 1) * 256]
            product = jnp.abs(dot(left, features, 1, 0))
            best = jnp.maximum(best, jnp.max(product.reshape(32, 8, 256), axis=0))
    out_ref[...] = jnp.maximum(before_ref[...], jnp.max(best))


def pick_kernel(at_ref, in_hbm, *refs):
    outs, (tokens, made, sems) = refs[:NZ], refs[NZ:]
    z, c, h = at_ref[0], at_ref[1], at_ref[2]
    load = pltpu.make_async_copy(in_hbm.at[pl.ds(pl.multiple_of(h * HALF, HALF), HALF)], tokens, sems.at[NZ])
    load.start()
    load.wait()
    sent = []
    for k in range(NZ):
        chip = lax.rem(z + (1 - 2 * c) * k + NZ, NZ)
        for j in range(2):
            side = c if j == 0 else 1 - c
            start = pl.multiple_of((chip * 2 + side) * OWN, LANES)
            made[k, :, j * OWN : (j + 1) * OWN] = tokens[:, pl.ds(start, OWN)]
        sent.append(pltpu.make_async_copy(made.at[k], outs[k], sems.at[k]))
        sent[-1].start()
    for copy in sent:
        copy.wait()


def stack_kernel(*refs):
    pieces, (out_ref, token_ref, sems) = refs[:NZ], refs[NZ:]
    copies = fetch([(piece, out_ref.at[k]) for k, piece in enumerate(pieces)], sems)
    token_ref[...] = jnp.zeros_like(token_ref)
    for copy in copies:
        copy.wait()


def tie_kernel(*refs):
    pass


def gate_kernel(*refs):
    refs[-1][...] = jnp.zeros_like(refs[-1])


def block_kernel(*refs):
    at_ref, chunks = refs[0], refs[1 : NT + 1]
    own_w, other_w, amax_ref, amax_other, out_hbm, rows, weights, made, sems, out_sems = refs[NT + 1 :]
    c = at_ref[1]
    copies = fetch(
        [(own_w, weights.at[0])]
        + [(chunk, rows.at[pl.ds(n * HALF, HALF)]) for n, chunk in enumerate(chunks)]
        + [(other_w, weights.at[1])],
        sems,
    )
    lanes = pieces_of(jnp.maximum(amax_ref[...], amax_other[...])[:1])
    for n in range(NT):
        for q in range(HALF // 16):
            made[n, q * 16 : q * 16 + 16, CHIP:] = lanes
    outs = []
    for j in range(2):
        copies[j * (NT + 1)].wait()
        for group in range(4):
            if j == 0:
                for n in range(4 * group, 4 * group + 4):
                    copies[1 + n].wait()
            left = rows[4 * group * HALF : 4 * (group + 1) * HALF]
            product = dot(left, weights[j], 1, 1).astype(jnp.bfloat16).reshape(4, HALF, OWN)
            made[4 * group : 4 * group + 4, :, j * OWN : (j + 1) * OWN] = product
            if j == 0:
                continue
            for k in (2 * group, 2 * group + 1):
                there = out_hbm.at[pl.ds(2 * block_of(c, k), 2)]
                outs.append(pltpu.make_async_copy(made.at[pl.ds(2 * k, 2)], there, out_sems.at[k]))
                outs[-1].start()
    for copy in outs:
        copy.wait()


def sum_kernel(in_ref, _, out_ref):
    total = in_ref[0, :, :CHIP].astype(jnp.float32)
    for n in range(1, NT):
        total = total + in_ref[n, :, :CHIP].astype(jnp.float32)
    out_ref[:, :CHIP] = total.astype(jnp.bfloat16)
    most = joined(in_ref[0, :16, CHIP:])
    for n in range(1, NT):
        most = jnp.maximum(most, joined(in_ref[n, :16, CHIP:]))
    for q in range(HALF // 16):
        out_ref[q * 16 : q * 16 + 16, CHIP:] = pieces_of(most)


def spread_kernel(in_ref, _, out_ref, token_ref):
    for n in range(NT):
        out_ref[n] = in_ref[...]
    token_ref[...] = jnp.zeros_like(token_ref)


def outer_kernel(at_ref, _, *refs):
    chunks = refs[:NT]
    mine_ref, theirs_ref, own_ref, other_ref, rows, left = refs[NT:]
    for n in range(NT):
        rows[n * HALF : (n + 1) * HALF] = chunks[n][...]
    for h, (one, two) in enumerate(((mine_ref, theirs_ref), (theirs_ref, mine_ref))):

        @pl.when(at_ref[2] == h)
        def _(one=one, two=two):
            for k in range(NZ):
                left[k * TOK_DEV : k * TOK_DEV + HALF] = one[k]
                left[k * TOK_DEV + HALF : (k + 1) * TOK_DEV] = two[k]

    other_ref[...] = dot(left[:, OWN:], rows[...], 0, 0).astype(jnp.bfloat16)
    own_ref[...] = dot(left[:, :OWN], rows[...], 0, 0).astype(jnp.bfloat16)


def final_kernel(
    at_ref, whole_hbm, own_hbm, come_hbm, gi_hbm, wg_hbm, amax_ref, whole, gi, own, come, made, sems
):
    whole_in, own_in, come_in = fetch([(whole_hbm, whole), (own_hbm, own), (come_hbm, come)], sems)
    z, c = at_ref[0], at_ref[1]
    whole_in.wait()
    most = joined(whole[0, :16, CHIP:])
    for n in range(1, NT):
        most = jnp.maximum(most, joined(whole[n, :16, CHIP:]))
    amax_ref[0, 0] = jnp.max(most)
    for k in range(NZ):
        chip = lax.rem(z + shift_of(c, k) + NZ, NZ)
        for j in range(2):
            side = c if j == 0 else 1 - c
            start = pl.multiple_of((chip * 2 + side) * OWN, LANES)
            for h in range(2):
                gi[h * HALF : (h + 1) * HALF, pl.ds(start, OWN)] = whole[2 * k + h, :, j * OWN : (j + 1) * OWN]
    outs = [pltpu.make_async_copy(gi, gi_hbm, sems.at[6])]
    outs[0].start()
    scale = 1.0 / (most[:, :1] + epsilon)
    own_in.wait()
    come_in.wait()
    for n in range(4):
        span = pl.ds(n * (OWN // 4), OWN // 4)
        made[span, :] = (own[span, :].astype(jnp.float32) + come[span, :].astype(jnp.float32)) * scale
        outs.append(pltpu.make_async_copy(made.at[span], wg_hbm.at[span], sems.at[2 + n]))
        outs[-1].start()
    for copy in outs:
        copy.wait()


def shape(dims, kind=jnp.bfloat16):
    return jax.ShapeDtypeStruct(dims, kind)


def cost(flops, moved):
    return pl.CostEstimate(flops=flops, bytes_accessed=moved, transcendentals=0)


def dma(count):
    return pltpu.SemaphoreType.DMA((count,))


AMAX_PARTS = 4


def call(kernel, in_specs, out_specs, out_shape, name, scratch=(), flops=0, moved=1 << 20, mib=56, **more):
    return pl.pallas_call(
        kernel,
        in_specs=in_specs,
        out_specs=out_specs,
        out_shape=out_shape,
        scratch_shapes=list(scratch),
        compiler_params=params(mib),
        cost_estimate=cost(flops, moved),
        name=name,
        **more,
    )


def tie(arrays, mib=4):
    count = len(arrays)
    return call(
        tie_kernel,
        [HBM] * count,
        [HBM] * count,
        [shape(array.shape, array.dtype) for array in arrays],
        "tie",
        mib=mib,
        input_output_aliases={n: n for n in range(count)},
    )(*arrays)


def gate(arrays):
    return call(gate_kernel, [HBM] * len(arrays), VMEM, shape((8, 128), jnp.float32), "gate")(*arrays)


def on_device(inputs, preact, grad_act, weight):
    d, t = lax.axis_index("dp"), lax.axis_index("tensor")
    place = jnp.stack([d // 2, d % 2, t % 2]).astype(jnp.int32)
    tile = shape((8, 128), jnp.float32)

    first, second = call(
        slope_kernel,
        [HBM] * 2,
        [VMEM] * 2,
        [shape((HALF, FF_DEV))] * 2,
        "slope",
        [pltpu.VMEM((TOK_DEV, FF_DEV), jnp.bfloat16)] * 2 + [dma(2)],
    )(preact, grad_act)
    other_w = lax.ppermute(weight, "dp", CORE_SWAP)

    chunks = {0: first, 1: second}

    def step(steps, h, *after):
        at = [((sign * (steps - 1)) % NZ) * 2 + h for sign in (1, -1)]
        if after:
            held = tie([chunks[n] for n in at] + list(after))
            chunks.update(zip(at, held))
            after = held[2:]
        for sign, n in zip((1, -1), at):
            if steps == 4 and (sign, h) in ((-1, 0), (1, 1)):
                continue
            chunks[((sign * steps) % NZ) * 2 + h] = lax.ppermute(chunks[n], "dp", ring_perm(sign))
        return after

    def amax_part(part, before):
        return call(
            functools.partial(amax_kernel, part),
            [VMEM] * 4,
            VMEM,
            tile,
            "amax",
            flops=2 * TOK_DEV * FF_DEV * D // AMAX_PARTS,
            mib=8,
        )(before, inputs, first, second)

    step(1, 0)
    step(1, 1)
    amax = amax_part(0, jnp.zeros((8, 128), jnp.float32))
    (amax,) = step(2, 0, amax)
    amax = amax_part(1, amax)
    (amax,) = step(2, 1, amax)
    amax = amax_part(2, amax)
    (amax,) = step(3, 0, amax)
    amax = amax_part(3, amax)
    (amax,) = step(3, 1, amax)
    amax_other = lax.ppermute(amax, "dp", CORE_SWAP)
    step(4, 0)
    step(4, 1)

    block = call(
        block_kernel,
        [SMEM] + [HBM] * (NT + 2) + [VMEM] * 2,
        HBM,
        shape((NT, HALF, WIDE)),
        "block",
        [
            pltpu.VMEM((NT * HALF, FF_DEV), jnp.bfloat16),
            pltpu.VMEM((2, OWN, FF_DEV), jnp.bfloat16),
            pltpu.VMEM((NT, HALF, WIDE), jnp.bfloat16),
            dma(NT + 2),
            dma(2 * NZ),
        ],
        2 * 1024 * FF_DEV * CHIP,
        7 << 20,
    )(place, *[chunks[n] for n in range(NT)], weight, other_w, amax, amax_other)
    swapped = lax.all_to_all(block, "tensor", 0, 0)

    pieces = call(
        pick_kernel,
        [SMEM, HBM],
        [HBM] * NZ,
        [shape((HALF, CHIP))] * NZ,
        "pick",
        [pltpu.VMEM((HALF, D), jnp.bfloat16), pltpu.VMEM((NZ, HALF, CHIP), jnp.bfloat16), dma(NZ + 1)],
    )(place, inputs)
    come_in = {0: pieces[0]}
    for k in (4, 3, 5, 2, 6, 1, 7):
        come_in[k] = lax.ppermute(pieces[k], "dp", ring_perm(k))
    mine, here = call(
        stack_kernel,
        [HBM] * NZ,
        [VMEM] * 2,
        [shape((NZ, HALF, CHIP)), tile],
        "stack",
        [dma(NZ)],
    )(*[come_in[k] for k in range(NZ)])
    theirs = lax.ppermute(mine, "tensor", [(n, n ^ 1) for n in range(NT)])
    early = gate([come_in[k] for k in (4, 3, 5)])
    summed = call(sum_kernel, [VMEM] * 2, VMEM, shape((HALF, WIDE)), "sum", mib=16)(swapped, early)
    back = lax.ppermute(summed, ("dp", "tensor"), spread_perm(-1))

    copies, token = call(
        spread_kernel, [VMEM] * 2, [VMEM] * 2, [shape((NT, HALF, WIDE)), tile], "spread", mib=16
    )(back, here)
    whole = lax.all_to_all(copies, "tensor", 0, 0)
    own, other = call(
        outer_kernel,
        [SMEM, VMEM] + [VMEM] * (NT + 2),
        [VMEM] * 2,
        [shape((OWN, FF_DEV))] * 2,
        "outer",
        [pltpu.VMEM((NT * HALF, FF_DEV), jnp.bfloat16), pltpu.VMEM((NT * HALF, CHIP), jnp.bfloat16)],
        2 * 1024 * FF_DEV * CHIP,
        9 << 20,
        mib=48,
    )(place, token, *[chunks[n] for n in range(NT)], mine, theirs)
    come = lax.ppermute(other, "dp", CORE_SWAP)
    grad_input, weight_grad, grad_amax = call(
        final_kernel,
        [SMEM, HBM, HBM, HBM],
        [HBM, HBM, SMEM],
        [shape((TOK_DEV, D)), shape((OWN, FF_DEV), jnp.float32), shape((1, 1), jnp.float32)],
        "final",
        [
            pltpu.VMEM((NT, HALF, WIDE), jnp.bfloat16),
            pltpu.VMEM((TOK_DEV, D), jnp.bfloat16),
            pltpu.VMEM((OWN, FF_DEV), jnp.bfloat16),
            pltpu.VMEM((OWN, FF_DEV), jnp.bfloat16),
            pltpu.VMEM((OWN, FF_DEV), jnp.float32),
            dma(7),
        ],
    )(place, whole, own, come)
    return (grad_input, weight_grad, grad_amax.reshape(()))


def solution(mesh):
    placed = (P("dp", None), P("dp", "tensor"), P("dp", "tensor"), P("dp", "tensor"))
    return jax.shard_map(
        on_device,
        mesh=mesh,
        in_specs=placed,
        out_specs=(P("dp", None), P("dp", "tensor"), P()),
        check_vma=False,
    )
```
